32 devices in a mesh: seq: 4 (over z), dp: 8 (over y, x, core).
Axes of the slice: x: 2, y: 2, z: 4, core: 2. Of those that a mesh axis runs over, the one named last changes fastest.
Arguments:
- tokens: bfloat16 [8, 1024, 768], P('dp', 'seq'), may hold values from -6 to 6
- qkv_weight: bfloat16 [768, 2304], P('dp'), may hold values from -0.21875 to 0.21875
- proj_weight: bfloat16 [768, 768], P('dp'), may hold values from -0.875 to 0.875
- hidden_weight: bfloat16 [768, 3072], P('dp'), may hold values from -0.21875 to 0.21875
- output_weight: bfloat16 [3072, 768], P('dp'), may hold values from -0.109375 to 0.109375
- first_gain: bfloat16 [768], P('dp'), may hold values from 0.25 to 1.75
- first_bias: bfloat16 [768], P('dp'), may hold values from -2.5 to 2.5
- second_gain: bfloat16 [768], P('dp'), may hold values from 0.25 to 1.75
- second_bias: bfloat16 [768], P('dp'), may hold values from -2.5 to 2.5
- cotangent: bfloat16 [8, 1024, 768], P('dp', 'seq'), may hold values from -6 to 6
Outputs:
- block_out: bfloat16 [8, 1024, 768], P('dp', 'seq')
- tokens_gradient: bfloat16 [8, 1024, 768], P('dp', 'seq')
- qkv_gradient: float32 [768, 2304], P('dp')
- proj_gradient: float32 [768, 768], P('dp')
- hidden_gradient: float32 [768, 3072], P('dp')
- output_gradient: float32 [3072, 768], P('dp')
- first_gain_gradient: float32 [768], P('dp')
- first_bias_gradient: float32 [768], P('dp')
- second_gain_gradient: float32 [768], P('dp')
- second_bias_gradient: float32 [768], P('dp')
The draws below stay inside these ranges and needn't reach their ends.
All inputs are finite; a program needn't handle non-finite values.
Results may differ from the reference program's by a relative error of at most 0.012.
Values may be sent and summed in bfloat16 or wider, within the bound.
A program may use at most 256 MiB of HBM per device.

```python
import jax
import jax.numpy as jnp
from jax import lax

D = 768
FF = 3072
HEADS = 12
HEAD_DIM = 64
SEQ_LEN = 1024
SEQS = 8


def level_of(rng, shape, pieces, low, top_value):
    def one(axis_at, parts):
        heights = jax.random.uniform(jax.random.fold_in(jax.random.fold_in(rng, 6), axis_at), (parts,), jnp.float32, low / len(pieces), top_value / len(pieces))
        return jnp.repeat(jnp.exp(heights), shape[axis_at] // parts).reshape((-1,) + (1,) * (len(shape) - axis_at - 1))

    factor_of = one(*pieces[0])
    for cut in pieces[1:]:
        factor_of = factor_of * one(*cut)
    return factor_of


def noise(own_key, dims, scale, bound, split=(), dtype=jnp.bfloat16):
    drawn = jax.random.normal(own_key, dims, jnp.float32) * scale
    if len(split) > 0:
        drawn = level_of(own_key, dims, split, -0.22, 0.18) * drawn
    return jnp.clip(drawn, min=-bound, max=bound).astype(dtype)


def setup_inputs(seed: int = 0) -> dict:
    arg_keys = jax.random.split(jax.random.key(seed), 11)
    tokens = noise(arg_keys[0], (SEQS, SEQ_LEN, D), 1.0, 6.0, ((0, 8), (1, 4)))
    qkv_weight = noise(arg_keys[1], (D, 3 * D), D ** -0.5, 0.21875, ((0, 8),))
    proj_weight = noise(arg_keys[2], (D, D), (D // 16) ** -0.5, 0.875, ((0, 8),))
    hidden_weight = noise(arg_keys[3], (D, FF), D ** -0.5, 0.21875, ((0, 8),))
    output_weight = noise(arg_keys[4], (FF, D), FF ** -0.5, 0.109375, ((0, 8),))
    first_gain = jnp.clip(1.0 + 0.15 * jax.random.normal(arg_keys[5], (D,), jnp.float32), 0.25, 1.75).astype(jnp.bfloat16)
    first_bias = noise(arg_keys[6], (D,), 0.3, 2.5, ((0, 8),))
    second_gain = jnp.clip(1.0 + 0.15 * jax.random.normal(arg_keys[7], (D,), jnp.float32), 0.25, 1.75).astype(jnp.bfloat16)
    second_bias = noise(arg_keys[8], (D,), 0.3, 2.5, ((0, 8),))
    cotangent = noise(arg_keys[9], (SEQS, SEQ_LEN, D), 1.0, 6.0, ((0, 8), (1, 4)))
    return {"tokens": tokens, "qkv_weight": qkv_weight, "proj_weight": proj_weight, "hidden_weight": hidden_weight, "output_weight": output_weight, "first_gain": first_gain, "first_bias": first_bias, "second_gain": second_gain, "second_bias": second_bias, "cotangent": cotangent}


@jax.custom_vjp
def low(v):
    return lax.optimization_barrier(v.astype(jnp.bfloat16)).astype(jnp.float32)

@jax.custom_vjp
def low_back(v):
    return v

def low_keep(v):
    return (low(v), None)

def low_pass(kept, grad):
    return (grad,)

def back_keep(v):
    return (v, None)

def back_low(kept, grad):
    return (low(grad),)
low.defvjp(low_keep, low_pass)
low_back.defvjp(back_keep, back_low)

def layer_norm(values, gain, bias):
    average = lax.optimization_barrier(jnp.mean(values, -1, keepdims=True))
    centred = values - average
    variance = lax.optimization_barrier(jnp.mean(centred * centred, -1, keepdims=True))
    return centred * lax.rsqrt(variance + 1e-05) * gain + bias

def matmul(left, right):
    return jnp.dot(left, right, precision=lax.Precision.HIGHEST, preferred_element_type=jnp.float32)

def attend(queries, keys, values):
    length = queries.shape[0]
    block_rows = min(512, length)
    blocks = length // block_rows
    scale = HEAD_DIM ** (-0.5)
    keys_split = keys.reshape(length, HEADS, HEAD_DIM)
    values_split = values.reshape(length, HEADS, HEAD_DIM)
    queries_split = queries.reshape(blocks, block_rows, HEADS, HEAD_DIM)
    starts = (jnp.arange(blocks) * block_rows).astype(jnp.int32)
    key_index = jnp.arange(length).astype(jnp.int32)

    def one_block(pair):
        query_block, first_row = pair
        raw = jnp.einsum('qhd,khd->hqk', query_block, keys_split, precision=lax.Precision.HIGHEST)
        positions = first_row + jnp.arange(block_rows).astype(jnp.int32)
        causal = key_index[None, :] <= positions[:, None]
        scores = low_back(jnp.where(causal[None], raw * scale, -1e+30))
        largest = lax.optimization_barrier(jnp.max(scores, -1, keepdims=True))
        expo = jnp.exp(scores - largest)
        probs = expo / lax.optimization_barrier(jnp.sum(expo, -1, keepdims=True))
        context = jnp.einsum('hqk,khd->qhd', low(probs), values_split, precision=lax.Precision.HIGHEST)
        return context.reshape(block_rows, HEADS * HEAD_DIM)
    outputs = lax.map(jax.checkpoint(one_block), (queries_split, starts))
    return outputs.reshape(length, HEADS * HEAD_DIM)

def layer(inputs, qkv_weight, proj_weight, hidden_weight, output_weight, first_gain, first_bias, second_gain, second_bias):
    width = inputs.shape[1]
    first_normed = low(layer_norm(inputs, first_gain, first_bias))
    projected = matmul(first_normed, qkv_weight)
    queries = low(low_back(projected[:, :width]))
    keys = low(low_back(projected[:, width:2 * width]))
    values = low(low_back(projected[:, 2 * width:]))
    context = low(low_back(attend(queries, keys, values)))
    attn = low_back(matmul(context, proj_weight))
    middle = inputs + attn
    second_normed = low(layer_norm(middle, second_gain, second_bias))
    hidden_pre = low_back(matmul(second_normed, hidden_weight))
    activated = low(jax.nn.gelu(hidden_pre, approximate=True))
    return middle + matmul(activated, output_weight)

def reference(tokens, qkv_weight, proj_weight, hidden_weight, output_weight, first_gain, first_bias, second_gain, second_bias, cotangent):
    params = tuple((item.astype(jnp.float32) for item in (qkv_weight, proj_weight, hidden_weight, output_weight, first_gain, first_bias, second_gain, second_bias)))
    inputs = tokens.astype(jnp.float32)
    checked = jax.checkpoint(layer)

    def whole(all_inputs, *weights):

        def one_sequence(carry, sequence):
            return (carry, checked(sequence, *weights))
        _, outputs = lax.scan(one_sequence, jnp.zeros((), jnp.float32), all_inputs)
        return outputs
    outputs, pullback = jax.vjp(whole, inputs, *params)
    grads = pullback(cotangent.astype(jnp.float32))
    return (outputs.astype(jnp.bfloat16), grads[0].astype(jnp.bfloat16), grads[1], grads[2], grads[3], grads[4], grads[5], grads[6], grads[7], grads[8])
```

```python
import jax
import jax.numpy as jnp
from jax import lax
from jax.sharding import PartitionSpec as P

HEAD_DIM = 64
LOW = jnp.bfloat16
F32 = jnp.float32


def layer_norm(values, gain, bias):
    average = jnp.mean(values, -1, keepdims=True)
    centred = values - average
    variance = jnp.mean(centred * centred, -1, keepdims=True)
    return centred * lax.rsqrt(variance + 1e-05) * gain + bias


def gelu_tanh(values):
    return jax.nn.gelu(values, approximate=True)


def matmul(left, right):
    return jnp.dot(left, right, preferred_element_type=F32)


def matmul_left_t(left, right):
    return lax.dot_general(left, right, (((0,), (0,)), ((), ())), preferred_element_type=F32)


def matmul_right_t(left, right):
    return lax.dot_general(left, right, (((1,), (1,)), ((), ())), preferred_element_type=F32)


def gather_seq(value):
    return lax.all_gather(value, "seq", axis=0, tiled=True)


def scatter_seq(value):
    return lax.psum_scatter(value.astype(LOW), "seq", scatter_dimension=0, tiled=True).astype(F32)


def attention_forward(queries, keys, values):
    length, local_width = queries.shape
    heads_here = local_width // HEAD_DIM
    block_rows = min(512, length)
    blocks = length // block_rows
    scale = HEAD_DIM ** (-0.5)
    outs, logs = [], []
    key_index = jnp.arange(length)
    for b in range(blocks):
        seen = (b + 1) * block_rows
        q = queries[b * block_rows : seen].reshape(block_rows, heads_here, HEAD_DIM)
        k = keys[:seen].reshape(seen, heads_here, HEAD_DIM)
        v = values[:seen].reshape(seen, heads_here, HEAD_DIM)
        raw = jnp.einsum("qhd,khd->hqk", q, k, preferred_element_type=F32)
        positions = b * block_rows + jnp.arange(block_rows)
        causal = key_index[None, :seen] <= positions[:, None]
        scores = jnp.where(causal[None], raw * scale, -1e30)
        largest = jnp.max(scores, -1, keepdims=True)
        expo = jnp.exp(scores - largest)
        total = jnp.sum(expo, -1, keepdims=True)
        probs = (expo / total).astype(LOW)
        context = jnp.einsum("hqk,khd->qhd", probs, v, preferred_element_type=F32)
        outs.append(context.astype(LOW).reshape(block_rows, local_width))
        logs.append(largest + jnp.log(total))
    return jnp.concatenate(outs, axis=0), logs


def attention_backward(queries, keys, values, grads, logs):
    length, local_width = queries.shape
    heads_here = local_width // HEAD_DIM
    block_rows = min(512, length)
    blocks = length // block_rows
    scale = HEAD_DIM ** (-0.5)
    key_index = jnp.arange(length)
    query_grads = []
    key_sum = jnp.zeros((length, heads_here, HEAD_DIM), F32)
    value_sum = jnp.zeros((length, heads_here, HEAD_DIM), F32)
    for b in range(blocks):
        seen = (b + 1) * block_rows
        q = queries[b * block_rows : seen].reshape(block_rows, heads_here, HEAD_DIM)
        g = grads[b * block_rows : seen].reshape(block_rows, heads_here, HEAD_DIM)
        k = keys[:seen].reshape(seen, heads_here, HEAD_DIM)
        v = values[:seen].reshape(seen, heads_here, HEAD_DIM)
        raw = jnp.einsum("qhd,khd->hqk", q, k, preferred_element_type=F32)
        positions = b * block_rows + jnp.arange(block_rows)
        causal = key_index[None, :seen] <= positions[:, None]
        scores = jnp.where(causal[None], raw * scale, -1e30)
        probs = jnp.exp(scores - logs[b])
        low_probs = probs.astype(LOW)
        value_term = jnp.einsum("hqk,qhd->khd", low_probs, g, preferred_element_type=F32)
        prob_grad = jnp.einsum("qhd,khd->hqk", g, v, preferred_element_type=F32)
        score_grad = (
            probs * (prob_grad - jnp.sum(probs * prob_grad, -1, keepdims=True))
        ).astype(LOW)
        query_grad = jnp.einsum("hqk,khd->qhd", score_grad, k, preferred_element_type=F32) * scale
        key_term = jnp.einsum("hqk,qhd->khd", score_grad, q, preferred_element_type=F32) * scale
        pad = ((0, length - seen), (0, 0), (0, 0))
        key_sum = key_sum + jnp.pad(key_term, pad)
        value_sum = value_sum + jnp.pad(value_term, pad)
        query_grads.append(query_grad.astype(LOW).reshape(block_rows, local_width))
    return (
        jnp.concatenate(query_grads, axis=0),
        key_sum.astype(LOW).reshape(length, local_width),
        value_sum.astype(LOW).reshape(length, local_width),
    )


def on_device(
    tokens,
    qkv_weight,
    proj_weight,
    hidden_weight,
    output_weight,
    first_gain,
    first_bias,
    second_gain,
    second_bias,
    cotangent,
):
    parts = lax.axis_size("seq")
    groups = lax.axis_size("dp")
    part = lax.axis_index("seq")
    inputs_low = tokens[0]
    rows, width = inputs_low.shape
    model_rows = qkv_weight.shape[0]
    local_width = width // parts
    hidden_rows = output_weight.shape[0] // parts
    hidden_here = hidden_rows * groups

    qkv_here = lax.dynamic_index_in_dim(
        qkv_weight.reshape(model_rows, 3, parts, local_width), part, 2, keepdims=False
    ).reshape(model_rows, 3 * local_width)
    hidden_cols = lax.dynamic_index_in_dim(
        hidden_weight.reshape(model_rows, groups, parts, hidden_rows), part, 2, keepdims=False
    ).reshape(model_rows, hidden_here)
    output_here = lax.dynamic_slice_in_dim(output_weight, part * hidden_rows, hidden_rows, 0)
    norms = jnp.stack([first_gain, first_bias, second_gain, second_bias], axis=0)
    norms = lax.all_gather(norms, "dp", axis=1, tiled=True).astype(F32)
    gain_one, bias_one, gain_two, bias_two = norms[0], norms[1], norms[2], norms[3]
    all_tokens = gather_seq(inputs_low)
    wide_qkv = lax.all_gather(qkv_here, "dp", axis=0, tiled=True)
    wide_proj = lax.all_gather(proj_weight, "dp", axis=0, tiled=True)
    wide_hidden = lax.all_gather(hidden_cols, "dp", axis=0, tiled=True)
    wide_output = lax.all_gather(output_here, "dp", axis=0, tiled=True)
    all_grads = gather_seq(cotangent[0])

    inputs = all_tokens.astype(F32)
    lowered_one = layer_norm(inputs, gain_one, bias_one).astype(LOW)
    projected = matmul(lowered_one, wide_qkv).astype(LOW)
    queries = projected[:, :local_width]
    keys = projected[:, local_width : 2 * local_width]
    values = projected[:, 2 * local_width :]
    context_here, logs = attention_forward(queries, keys, values)
    context = lax.all_gather(context_here, "seq", axis=1, tiled=True)
    middle = inputs + matmul(context, wide_proj)
    lowered_two = layer_norm(middle, gain_two, bias_two).astype(LOW)
    hidden_pre = matmul(lowered_two, wide_hidden)
    activated_float, gelu_pull = jax.vjp(gelu_tanh, hidden_pre)
    activated = activated_float.astype(LOW)

    act_grad = matmul_right_t(all_grads, wide_output)
    pre_grad = gelu_pull(act_grad)[0].astype(LOW)
    normed_two_grad = scatter_seq(matmul_right_t(pre_grad, wide_hidden))
    ffn_out = scatter_seq(matmul(activated, wide_output))
    middle_own = lax.dynamic_slice_in_dim(middle, part * rows, rows, 0)
    block_out = middle_own + ffn_out
    _, norm_pull_two = jax.vjp(layer_norm, middle_own, gain_two, bias_two)
    middle_part, gain_two_term, bias_two_term = norm_pull_two(normed_two_grad)
    middle_grad = cotangent[0].astype(F32) + middle_part
    attn_grad = gather_seq(middle_grad.astype(LOW))

    proj_here = lax.dynamic_slice_in_dim(wide_proj, part * local_width, local_width, 0)
    context_grad = matmul_right_t(attn_grad, proj_here).astype(LOW)
    query_grads, key_grads, value_grads = attention_backward(
        queries, keys, values, context_grad, logs
    )
    qkv_grad = jnp.concatenate([query_grads, key_grads, value_grads], axis=1)
    normed_one_grad = scatter_seq(matmul_right_t(qkv_grad, wide_qkv))
    _, norm_pull_one = jax.vjp(layer_norm, inputs_low.astype(F32), gain_one, bias_one)
    input_part, gain_one_term, bias_one_term = norm_pull_one(normed_one_grad)
    tokens_gradient = (middle_grad + input_part).astype(LOW)

    attn_cols = lax.dynamic_slice_in_dim(attn_grad, part * local_width, local_width, 1)
    output_term = matmul_left_t(activated, all_grads).astype(LOW)
    hidden_term = matmul_left_t(lowered_two, pre_grad).astype(LOW)
    proj_term = matmul_left_t(context, attn_cols).astype(LOW)
    qkv_term = matmul_left_t(lowered_one, qkv_grad).astype(LOW)
    first_terms = jnp.concatenate([output_term, hidden_term], axis=1)
    second_terms = jnp.concatenate([proj_term, qkv_term], axis=1)
    first_sum = lax.psum_scatter(first_terms, "dp", scatter_dimension=0, tiled=True)
    second_sum = lax.psum_scatter(second_terms, "dp", scatter_dimension=0, tiled=True)
    first_all = lax.all_gather(first_sum, "seq", axis=0)
    second_all = lax.all_gather(second_sum, "seq", axis=0)
    output_gradient = first_all[:, :, :width].reshape(parts * hidden_rows, width).astype(F32)
    hidden_gradient = (
        first_all[:, :, width:]
        .reshape(parts, model_rows, groups, hidden_rows)
        .transpose(1, 2, 0, 3)
        .reshape(model_rows, parts * hidden_here)
        .astype(F32)
    )
    proj_gradient = (
        second_all[:, :, :local_width].transpose(1, 0, 2).reshape(model_rows, width).astype(F32)
    )
    qkv_gradient = (
        second_all[:, :, local_width:]
        .reshape(parts, model_rows, 3, local_width)
        .transpose(1, 2, 0, 3)
        .reshape(model_rows, 3 * width)
        .astype(F32)
    )
    norm_terms = jnp.stack([gain_one_term, bias_one_term, gain_two_term, bias_two_term], axis=0)
    norm_sum = lax.psum(norm_terms, ("seq", "dp"))
    norm_own = lax.dynamic_slice_in_dim(
        norm_sum, lax.axis_index("dp") * first_gain.shape[0], first_gain.shape[0], 1
    )
    return (
        block_out.astype(LOW)[None],
        tokens_gradient[None],
        qkv_gradient,
        proj_gradient,
        hidden_gradient,
        output_gradient,
        norm_own[0],
        norm_own[1],
        norm_own[2],
        norm_own[3],
    )


def solution(mesh):
    placed = (
        P("dp", "seq", None),
        P("dp", None),
        P("dp", None),
        P("dp", None),
        P("dp", None),
        P("dp"),
        P("dp"),
        P("dp"),
        P("dp"),
        P("dp", "seq", None),
    )
    return jax.shard_map(
        on_device,
        mesh=mesh,
        in_specs=placed,
        out_specs=(
            P("dp", "seq", None),
            P("dp", "seq", None),
            P("dp", None),
            P("dp", None),
            P("dp", None),
            P("dp", None),
            P("dp"),
            P("dp"),
            P("dp"),
            P("dp"),
        ),
        check_vma=False,
    )
```

```python
import jax
import jax.numpy as jnp
from jax import lax
from jax.experimental import pallas as pl
from jax.experimental.pallas import tpu as pltpu
from jax.sharding import PartitionSpec as P

HEAD_DIM = 64
LOW = jnp.bfloat16
F32 = jnp.float32


def layer_norm(values, gain, bias):
    average = jnp.mean(values, -1, keepdims=True)
    centred = values - average
    variance = jnp.mean(centred * centred, -1, keepdims=True)
    return centred * lax.rsqrt(variance + 1e-05) * gain + bias


def gelu_tanh(values):
    return jax.nn.gelu(values, approximate=True)


def matmul(left, right):
    return jnp.dot(left, right, preferred_element_type=F32)


def matmul_left_t(left, right):
    return lax.dot_general(left, right, (((0,), (0,)), ((), ())), preferred_element_type=F32)


def matmul_right_t(left, right):
    return lax.dot_general(left, right, (((1,), (1,)), ((), ())), preferred_element_type=F32)


def gather_seq(value):
    return lax.all_gather(value, "seq", axis=0, tiled=True)


def scatter_seq(value):
    return lax.psum_scatter(value.astype(LOW), "seq", scatter_dimension=0, tiled=True).astype(F32)


def remote(src, dst, send, recv, axis, target):
    return pltpu.make_async_remote_copy(
        src_ref=src,
        dst_ref=dst,
        send_sem=send,
        recv_sem=recv,
        device_id={axis: target},
        device_id_type=pl.DeviceIdType.MESH,
    )


def greet(axes):
    barrier = pltpu.get_barrier_semaphore()
    count = 0
    for axis, size in axes:
        me = lax.axis_index(axis)
        for step in range(1, size):
            pl.semaphore_signal(
                barrier,
                inc=1,
                device_id={axis: lax.rem(me + step, size)},
                device_id_type=pl.DeviceIdType.MESH,
            )
            count += 1
    pl.semaphore_wait(barrier, count)


ANY = pl.BlockSpec(memory_space=pl.ANY)
VMEM = pl.BlockSpec(memory_space=pltpu.VMEM)


def params(collective_id):
    return pltpu.CompilerParams(
        collective_id=collective_id, has_side_effects=True, vmem_limit_bytes=32 * 1024 * 1024
    )


def start_gather(parts, groups, tokens, pieces):
    count = len(pieces)
    half = groups // 2

    def kernel(*refs):
        token_in, piece_in = refs[0], refs[1 : 1 + count]
        token_out, piece_out = refs[1 + count], refs[2 + count : 2 + 2 * count]
        token_send, token_recv, send, recv, pair_send, pair_recv, own = refs[2 + 2 * count :]
        seq, dp = lax.axis_index("seq"), lax.axis_index("dp")
        sibling = dp + 1 - 2 * lax.rem(dp, 2)
        greet((("seq", parts), ("dp", groups)))
        far, near, token_copies, local = [], [], [], []
        for k in range(count):
            for step in range(1, half):
                copy = remote(
                    piece_in[k],
                    piece_out[k].at[dp],
                    send.at[k, step],
                    recv.at[k, step],
                    "dp",
                    lax.rem(dp + 2 * step, groups),
                )
                copy.start()
                far.append((k, step, copy))
        for step in range(1, parts):
            copy = remote(
                token_in,
                token_out.at[seq],
                token_send.at[step],
                token_recv.at[step],
                "seq",
                lax.rem(seq + step, parts),
            )
            copy.start()
            token_copies.append(copy)
        for k in range(count):
            copy = remote(
                piece_in[k],
                piece_out[k].at[dp],
                pair_send.at[k, 0],
                pair_recv.at[k, 0],
                "dp",
                sibling,
            )
            copy.start()
            near.append(copy)
            copy = pltpu.make_async_copy(piece_in[k], piece_out[k].at[dp], own.at[k])
            copy.start()
            local.append(copy)
        copy = pltpu.make_async_copy(token_in, token_out.at[seq], own.at[count])
        copy.start()
        local.append(copy)
        for k, step, copy in far:
            copy.wait_recv()
            origin = lax.rem(dp - 2 * step + groups, groups)
            passed = remote(
                piece_out[k].at[origin],
                piece_out[k].at[origin],
                pair_send.at[k, step],
                pair_recv.at[k, step],
                "dp",
                sibling,
            )
            passed.start()
            near.append(passed)
        for _, _, copy in far:
            copy.wait_send()
        for copy in near + token_copies + local:
            copy.wait()

    return pl.pallas_call(
        kernel,
        out_shape=[jax.ShapeDtypeStruct((parts,) + tokens.shape, tokens.dtype)]
        + [jax.ShapeDtypeStruct((groups,) + item.shape, item.dtype) for item in pieces],
        in_specs=[ANY] * (1 + count),
        out_specs=[ANY] * (1 + count),
        scratch_shapes=[
            pltpu.SemaphoreType.DMA((parts,)),
            pltpu.SemaphoreType.DMA((parts,)),
            pltpu.SemaphoreType.DMA((count, half)),
            pltpu.SemaphoreType.DMA((count, half)),
            pltpu.SemaphoreType.DMA((count, half)),
            pltpu.SemaphoreType.DMA((count, half)),
            pltpu.SemaphoreType.DMA((count + 1,)),
        ],
        compiler_params=params(0),
        name="start_gather",
    )(tokens, *pieces)


def seq_kernel(parts, value, exchange, collective_id, name):
    piece = value.shape[1:] if exchange else value.shape

    def kernel(in_ref, out_ref, send, recv, own):
        seq = lax.axis_index("seq")
        greet((("seq", parts),))
        copies = []
        for step in range(1, parts):
            target = lax.rem(seq + step, parts)
            copy = remote(
                in_ref.at[target] if exchange else in_ref,
                out_ref.at[seq],
                send.at[step],
                recv.at[step],
                "seq",
                target,
            )
            copy.start()
            copies.append(copy)
        copy = pltpu.make_async_copy(
            in_ref.at[seq] if exchange else in_ref, out_ref.at[seq], own
        )
        copy.start()
        for item in copies + [copy]:
            item.wait()

    return pl.pallas_call(
        kernel,
        out_shape=jax.ShapeDtypeStruct((parts,) + piece, value.dtype),
        in_specs=[ANY],
        out_specs=ANY,
        scratch_shapes=[
            pltpu.SemaphoreType.DMA((parts,)),
            pltpu.SemaphoreType.DMA((parts,)),
            pltpu.SemaphoreType.DMA,
        ],
        compiler_params=params(collective_id),
        name=name,
    )(value)


def last_exchange(parts, groups, partial, terms):
    block = terms.shape[1:]

    def kernel(
        partial_in, terms_in, partial_out, sums_out, land, total, seq_send, seq_recv, send, recv,
        sum_send, sum_recv, own
    ):
        seq, dp = lax.axis_index("seq"), lax.axis_index("dp")
        greet((("seq", parts), ("dp", groups)))
        dp_copies, seq_copies = [], []
        for step in range(1, groups):
            target = lax.rem(dp + step, groups)
            copy = remote(
                terms_in.at[target], land.at[dp], send.at[step], recv.at[step], "dp", target
            )
            copy.start()
            dp_copies.append(copy)
        for step in range(1, parts):
            target = lax.rem(seq + step, parts)
            copy = remote(
                partial_in.at[target],
                partial_out.at[seq],
                seq_send.at[step],
                seq_recv.at[step],
                "seq",
                target,
            )
            copy.start()
            seq_copies.append(copy)
        own_copy = pltpu.make_async_copy(partial_in.at[seq], partial_out.at[seq], own.at[0])
        own_copy.start()
        for copy in dp_copies:
            copy.wait()
        summed = terms_in[dp].astype(F32)
        for step in range(1, groups):
            summed = summed + land[lax.rem(dp + step, groups)].astype(F32)
        total[...] = summed.astype(LOW)
        for step in range(1, parts):
            copy = remote(
                total,
                sums_out.at[seq],
                sum_send.at[step],
                sum_recv.at[step],
                "seq",
                lax.rem(seq + step, parts),
            )
            copy.start()
            seq_copies.append(copy)
        sum_copy = pltpu.make_async_copy(total, sums_out.at[seq], own.at[1])
        sum_copy.start()
        for copy in seq_copies + [own_copy, sum_copy]:
            copy.wait()

    dma = pltpu.SemaphoreType.DMA
    return pl.pallas_call(
        kernel,
        out_shape=[
            jax.ShapeDtypeStruct(partial.shape, partial.dtype),
            jax.ShapeDtypeStruct((parts,) + block, terms.dtype),
        ],
        in_specs=[ANY, VMEM],
        out_specs=[ANY, ANY],
        scratch_shapes=[
            pltpu.VMEM(terms.shape, terms.dtype),
            pltpu.VMEM(block, terms.dtype),
            dma((parts,)),
            dma((parts,)),
            dma((groups,)),
            dma((groups,)),
            dma((parts,)),
            dma((parts,)),
            dma((2,)),
        ],
        compiler_params=params(4),
        name="last_exchange",
    )(partial, terms)


def norm_reduce(parts, groups, terms):
    block = terms.shape[1:]

    def kernel(terms_in, out, land, total, seq_land, send, recv, seq_send, seq_recv):
        seq, dp = lax.axis_index("seq"), lax.axis_index("dp")
        greet((("seq", parts), ("dp", groups)))
        copies = []
        for step in range(1, groups):
            target = lax.rem(dp + step, groups)
            copy = remote(
                terms_in.at[target], land.at[dp], send.at[step], recv.at[step], "dp", target
            )
            copy.start()
            copies.append(copy)
        for copy in copies:
            copy.wait()
        summed = terms_in[dp]
        for step in range(1, groups):
            summed = summed + land[lax.rem(dp + step, groups)]
        total[...] = summed
        copies = []
        for step in range(1, parts):
            copy = remote(
                total,
                seq_land.at[seq],
                seq_send.at[step],
                seq_recv.at[step],
                "seq",
                lax.rem(seq + step, parts),
            )
            copy.start()
            copies.append(copy)
        for copy in copies:
            copy.wait()
        for step in range(1, parts):
            summed = summed + seq_land[lax.rem(seq + step, parts)]
        out[...] = summed

    dma = pltpu.SemaphoreType.DMA
    return pl.pallas_call(
        kernel,
        out_shape=jax.ShapeDtypeStruct(block, terms.dtype),
        in_specs=[VMEM],
        out_specs=VMEM,
        scratch_shapes=[
            pltpu.VMEM(terms.shape, terms.dtype),
            pltpu.VMEM(block, terms.dtype),
            pltpu.VMEM((parts,) + block, terms.dtype),
            dma((groups,)),
            dma((groups,)),
            dma((parts,)),
            dma((parts,)),
        ],
        compiler_params=params(5),
        name="norm_reduce",
    )(terms)


def attention_forward(queries, keys, values):
    length, local_width = queries.shape
    heads_here = local_width // HEAD_DIM
    block_rows = min(512, length)
    blocks = length // block_rows
    scale = HEAD_DIM ** (-0.5)
    outs, logs = [], []
    key_index = jnp.arange(length)
    for b in range(blocks):
        seen = (b + 1) * block_rows
        q = queries[b * block_rows : seen].reshape(block_rows, heads_here, HEAD_DIM)
        k = keys[:seen].reshape(seen, heads_here, HEAD_DIM)
        v = values[:seen].reshape(seen, heads_here, HEAD_DIM)
        raw = jnp.einsum("qhd,khd->hqk", q, k, preferred_element_type=F32)
        positions = b * block_rows + jnp.arange(block_rows)
        causal = key_index[None, :seen] <= positions[:, None]
        scores = jnp.where(causal[None], raw * scale, -1e30)
        largest = jnp.max(scores, -1, keepdims=True)
        expo = jnp.exp(scores - largest)
        total = jnp.sum(expo, -1, keepdims=True)
        probs = (expo / total).astype(LOW)
        context = jnp.einsum("hqk,khd->qhd", probs, v, preferred_element_type=F32)
        outs.append(context.astype(LOW).reshape(block_rows, local_width))
        logs.append(largest + jnp.log(total))
    return jnp.concatenate(outs, axis=0), logs


def attention_backward(queries, keys, values, grads, logs):
    length, local_width = queries.shape
    heads_here = local_width // HEAD_DIM
    block_rows = min(512, length)
    blocks = length // block_rows
    scale = HEAD_DIM ** (-0.5)
    key_index = jnp.arange(length)
    query_grads = []
    key_sum = jnp.zeros((length, heads_here, HEAD_DIM), F32)
    value_sum = jnp.zeros((length, heads_here, HEAD_DIM), F32)
    for b in range(blocks):
        seen = (b + 1) * block_rows
        q = queries[b * block_rows : seen].reshape(block_rows, heads_here, HEAD_DIM)
        g = grads[b * block_rows : seen].reshape(block_rows, heads_here, HEAD_DIM)
        k = keys[:seen].reshape(seen, heads_here, HEAD_DIM)
        v = values[:seen].reshape(seen, heads_here, HEAD_DIM)
        raw = jnp.einsum("qhd,khd->hqk", q, k, preferred_element_type=F32)
        positions = b * block_rows + jnp.arange(block_rows)
        causal = key_index[None, :seen] <= positions[:, None]
        scores = jnp.where(causal[None], raw * scale, -1e30)
        probs = jnp.exp(scores - logs[b])
        low_probs = probs.astype(LOW)
        value_term = jnp.einsum("hqk,qhd->khd", low_probs, g, preferred_element_type=F32)
        prob_grad = jnp.einsum("qhd,khd->hqk", g, v, preferred_element_type=F32)
        score_grad = (
            probs * (prob_grad - jnp.sum(probs * prob_grad, -1, keepdims=True))
        ).astype(LOW)
        query_grad = jnp.einsum("hqk,khd->qhd", score_grad, k, preferred_element_type=F32) * scale
        key_term = jnp.einsum("hqk,qhd->khd", score_grad, q, preferred_element_type=F32) * scale
        pad = ((0, length - seen), (0, 0), (0, 0))
        key_sum = key_sum + jnp.pad(key_term, pad)
        value_sum = value_sum + jnp.pad(value_term, pad)
        query_grads.append(query_grad.astype(LOW).reshape(block_rows, local_width))
    return (
        jnp.concatenate(query_grads, axis=0),
        key_sum.astype(LOW).reshape(length, local_width),
        value_sum.astype(LOW).reshape(length, local_width),
    )


def on_device(
    tokens,
    qkv_weight,
    proj_weight,
    hidden_weight,
    output_weight,
    first_gain,
    first_bias,
    second_gain,
    second_bias,
    cotangent,
):
    parts = lax.axis_size("seq")
    groups = lax.axis_size("dp")
    part = lax.axis_index("seq")
    inputs_low = tokens[0]
    rows, width = inputs_low.shape
    model_rows = qkv_weight.shape[0]
    local_width = width // parts
    hidden_rows = output_weight.shape[0] // parts
    hidden_here = hidden_rows * groups

    qkv_here = lax.dynamic_index_in_dim(
        qkv_weight.reshape(model_rows, 3, parts, local_width), part, 2, keepdims=False
    ).reshape(model_rows, 3 * local_width)
    hidden_cols = lax.dynamic_index_in_dim(
        hidden_weight.reshape(model_rows, groups, parts, hidden_rows), part, 2, keepdims=False
    ).reshape(model_rows, hidden_here)
    output_here = lax.dynamic_slice_in_dim(output_weight, part * hidden_rows, hidden_rows, 0)
    direct = model_rows % 16 == 0 and rows % 16 == 0 and groups % 2 == 0
    norms = jnp.stack([first_gain, first_bias, second_gain, second_bias], axis=0)
    if direct:
        pad_lanes = -first_gain.shape[0] % 128
        padded = jnp.pad(norms.astype(F32), ((0, 4), (0, pad_lanes)))
        all_tokens, *pieces = start_gather(
            parts,
            groups,
            inputs_low,
            (qkv_here, padded, proj_weight, hidden_cols, output_here),
        )
        wide_qkv, wide_proj, wide_hidden, wide_output = [
            pieces[at].reshape(groups * pieces[at].shape[1], pieces[at].shape[2])
            for at in (0, 2, 3, 4)
        ]
        norms = pieces[1][:, :4, : first_gain.shape[0]].transpose(1, 0, 2).reshape(4, width)
        all_tokens = all_tokens.reshape(parts * rows, width)
        own_grads, all_tokens = lax.optimization_barrier((cotangent[0], all_tokens))
        all_grads = gather_seq(own_grads)
    else:
        norms = lax.all_gather(norms, "dp", axis=1, tiled=True).astype(F32)
        all_tokens = gather_seq(inputs_low)
        wide_qkv = lax.all_gather(qkv_here, "dp", axis=0, tiled=True)
        wide_proj = lax.all_gather(proj_weight, "dp", axis=0, tiled=True)
        wide_hidden = lax.all_gather(hidden_cols, "dp", axis=0, tiled=True)
        wide_output = lax.all_gather(output_here, "dp", axis=0, tiled=True)
        all_grads = gather_seq(cotangent[0])
    gain_one, bias_one, gain_two, bias_two = norms[0], norms[1], norms[2], norms[3]

    inputs = all_tokens.astype(F32)
    lowered_one = layer_norm(inputs, gain_one, bias_one).astype(LOW)
    projected = matmul(lowered_one, wide_qkv).astype(LOW)
    queries = projected[:, :local_width]
    keys = projected[:, local_width : 2 * local_width]
    values = projected[:, 2 * local_width :]
    context_here, logs = attention_forward(queries, keys, values)
    if direct:
        context = seq_kernel(parts, context_here, False, 1, "context_gather")
        context = context.transpose(1, 0, 2).reshape(parts * rows, width)
    else:
        context = lax.all_gather(context_here, "seq", axis=1, tiled=True)
    middle = inputs + matmul(context, wide_proj)
    lowered_two = layer_norm(middle, gain_two, bias_two).astype(LOW)
    hidden_pre = matmul(lowered_two, wide_hidden)
    activated_float, gelu_pull = jax.vjp(gelu_tanh, hidden_pre)
    activated = activated_float.astype(LOW)

    act_grad = matmul_right_t(all_grads, wide_output)
    pre_grad = gelu_pull(act_grad)[0].astype(LOW)
    normed_two_grad = matmul_right_t(pre_grad, wide_hidden)
    if direct:
        normed_two_grad = seq_kernel(
            parts,
            normed_two_grad.astype(LOW).reshape(parts, rows, width),
            True,
            2,
            "hidden_exchange",
        )
        normed_two_grad = jnp.sum(normed_two_grad.astype(F32), axis=0)
    else:
        normed_two_grad = scatter_seq(normed_two_grad)
    ffn_out = scatter_seq(matmul(activated, wide_output))
    middle_own = lax.dynamic_slice_in_dim(middle, part * rows, rows, 0)
    block_out = middle_own + ffn_out
    _, norm_pull_two = jax.vjp(layer_norm, middle_own, gain_two, bias_two)
    middle_part, gain_two_term, bias_two_term = norm_pull_two(normed_two_grad)
    middle_grad = cotangent[0].astype(F32) + middle_part
    if direct:
        attn_grad = seq_kernel(parts, middle_grad.astype(LOW), False, 3, "attn_gather")
        attn_grad = attn_grad.reshape(parts * rows, width)
    else:
        attn_grad = gather_seq(middle_grad.astype(LOW))

    proj_here = lax.dynamic_slice_in_dim(wide_proj, part * local_width, local_width, 0)
    context_grad = matmul_right_t(attn_grad, proj_here).astype(LOW)
    query_grads, key_grads, value_grads = attention_backward(
        queries, keys, values, context_grad, logs
    )
    qkv_grad = jnp.concatenate([query_grads, key_grads, value_grads], axis=1)
    attn_cols = lax.dynamic_slice_in_dim(attn_grad, part * local_width, local_width, 1)
    proj_term = matmul_left_t(context, attn_cols).astype(LOW)
    qkv_term = matmul_left_t(lowered_one, qkv_grad).astype(LOW)
    second_terms = jnp.concatenate([proj_term, qkv_term], axis=1)
    normed_one_grad = matmul_right_t(qkv_grad, wide_qkv)
    if direct:
        normed_one_grad, second_all = last_exchange(
            parts,
            groups,
            normed_one_grad.astype(LOW).reshape(parts, rows, width),
            second_terms.reshape(groups, model_rows, second_terms.shape[1]),
        )
        normed_one_grad = jnp.sum(normed_one_grad.astype(F32), axis=0)
    else:
        normed_one_grad = scatter_seq(normed_one_grad)
        second_sum = lax.psum_scatter(second_terms, "dp", scatter_dimension=0, tiled=True)
        second_all = lax.all_gather(second_sum, "seq", axis=0)
    _, norm_pull_one = jax.vjp(layer_norm, inputs_low.astype(F32), gain_one, bias_one)
    input_part, gain_one_term, bias_one_term = norm_pull_one(normed_one_grad)
    tokens_gradient = (middle_grad + input_part).astype(LOW)

    output_term = matmul_left_t(activated, all_grads).astype(LOW)
    hidden_term = matmul_left_t(lowered_two, pre_grad).astype(LOW)
    first_terms = jnp.concatenate([output_term, hidden_term], axis=1)
    first_sum = lax.psum_scatter(first_terms, "dp", scatter_dimension=0, tiled=True)
    first_all = lax.all_gather(first_sum, "seq", axis=0)
    output_gradient = first_all[:, :, :width].reshape(parts * hidden_rows, width).astype(F32)
    hidden_gradient = (
        first_all[:, :, width:]
        .reshape(parts, model_rows, groups, hidden_rows)
        .transpose(1, 2, 0, 3)
        .reshape(model_rows, parts * hidden_here)
        .astype(F32)
    )
    proj_gradient = (
        second_all[:, :, :local_width].transpose(1, 0, 2).reshape(model_rows, width).astype(F32)
    )
    qkv_gradient = (
        second_all[:, :, local_width:]
        .reshape(parts, model_rows, 3, local_width)
        .transpose(1, 2, 0, 3)
        .reshape(model_rows, 3 * width)
        .astype(F32)
    )
    norm_terms = jnp.stack([gain_one_term, bias_one_term, gain_two_term, bias_two_term], axis=0)
    if direct:
        norm_blocks = norm_terms.reshape(4, groups, model_rows).transpose(1, 0, 2)
        norm_blocks = jnp.pad(norm_blocks, ((0, 0), (0, 4), (0, -model_rows % 128)))
        norm_own = norm_reduce(parts, groups, norm_blocks)[:4, :model_rows]
    else:
        norm_sum = lax.psum(norm_terms, ("seq", "dp"))
        norm_own = lax.dynamic_slice_in_dim(
            norm_sum, lax.axis_index("dp") * model_rows, model_rows, 1
        )
    return (
        block_out.astype(LOW)[None],
        tokens_gradient[None],
        qkv_gradient,
        proj_gradient,
        hidden_gradient,
        output_gradient,
        norm_own[0],
        norm_own[1],
        norm_own[2],
        norm_own[3],
    )


def solution(mesh):
    placed = (
        P("dp", "seq", None),
        P("dp", None),
        P("dp", None),
        P("dp", None),
        P("dp", None),
        P("dp"),
        P("dp"),
        P("dp"),
        P("dp"),
        P("dp", "seq", None),
    )
    return jax.shard_map(
        on_device,
        mesh=mesh,
        in_specs=placed,
        out_specs=(
            P("dp", "seq", None),
            P("dp", "seq", None),
            P("dp", None),
            P("dp", None),
            P("dp", None),
            P("dp", None),
            P("dp"),
            P("dp"),
            P("dp"),
            P("dp"),
        ),
        check_vma=False,
    )
```

```python
import jax
import jax.numpy as jnp
from jax import lax
from jax.experimental import pallas as pl
from jax.experimental.pallas import tpu as pltpu
from jax.sharding import PartitionSpec as P

HEAD_DIM = 64
LOW = jnp.bfloat16
F32 = jnp.float32


def layer_norm(values, gain, bias):
    average = jnp.mean(values, -1, keepdims=True)
    centred = values - average
    variance = jnp.mean(centred * centred, -1, keepdims=True)
    return centred * lax.rsqrt(variance + 1e-05) * gain + bias


def gelu_tanh(values):
    return jax.nn.gelu(values, approximate=True)


def matmul(left, right):
    return jnp.dot(left, right, preferred_element_type=F32)


def matmul_left_t(left, right):
    return lax.dot_general(left, right, (((0,), (0,)), ((), ())), preferred_element_type=F32)


def matmul_right_t(left, right):
    return lax.dot_general(left, right, (((1,), (1,)), ((), ())), preferred_element_type=F32)


def gather_seq(value):
    return lax.all_gather(value, "seq", axis=0, tiled=True)


def scatter_seq(value):
    return lax.psum_scatter(value.astype(LOW), "seq", scatter_dimension=0, tiled=True).astype(F32)


def remote(src, dst, send, recv, axis, target):
    return pltpu.make_async_remote_copy(
        src_ref=src,
        dst_ref=dst,
        send_sem=send,
        recv_sem=recv,
        device_id={axis: target},
        device_id_type=pl.DeviceIdType.MESH,
    )


def greet(axes):
    barrier = pltpu.get_barrier_semaphore()
    count = 0
    for axis, size in axes:
        me = lax.axis_index(axis)
        for step in range(1, size):
            pl.semaphore_signal(
                barrier,
                inc=1,
                device_id={axis: lax.rem(me + step, size)},
                device_id_type=pl.DeviceIdType.MESH,
            )
            count += 1
    pl.semaphore_wait(barrier, count)


ANY = pl.BlockSpec(memory_space=pl.ANY)
VMEM = pl.BlockSpec(memory_space=pltpu.VMEM)


def params(collective_id):
    return pltpu.CompilerParams(
        collective_id=collective_id, has_side_effects=True, vmem_limit_bytes=32 * 1024 * 1024
    )


def line_gather(parts, source, out, send, recv, own):
    seq = lax.axis_index("seq")
    local = pltpu.make_async_copy(source, out.at[seq], own)
    local.start()

    def hop(way, sign, step):
        origin = lax.rem(seq - sign * step + parts, parts)
        return remote(
            source if step == 0 else out.at[origin],
            out.at[origin],
            send.at[way, step],
            recv.at[way, step],
            "seq",
            lax.rem(seq + sign + parts, parts),
        )

    def sends(sign, step):
        origin = seq - sign * step
        return (seq + sign >= 0) & (seq + sign < parts) & (origin >= 0) & (origin < parts)

    def arrives(sign, step):
        origin = seq - sign * step
        return (origin >= 0) & (origin < parts)

    ways = ((0, 1), (1, -1))
    for way, sign in ways:

        @pl.when(sends(sign, 0))
        def _():
            hop(way, sign, 0).start()

    yield
    for step in range(1, parts):
        for way, sign in ways:

            @pl.when(arrives(sign, step))
            def _():
                origin = lax.rem(seq - sign * step + parts, parts)
                remote(
                    source,
                    out.at[origin],
                    send.at[way, step - 1],
                    recv.at[way, step - 1],
                    "seq",
                    lax.rem(seq + sign + parts, parts),
                ).wait_recv()

            if step < parts - 1:

                @pl.when(sends(sign, step))
                def _():
                    hop(way, sign, step).start()

    yield
    for step in range(parts - 1):
        for way, sign in ways:

            @pl.when(sends(sign, step))
            def _():
                hop(way, sign, step).wait_send()

    local.wait()


def line_reduce(parts, terms, out, stage, land, send, recv):
    seq = lax.axis_index("seq")
    signs = (1, -1)

    def copy(way, dest):
        return remote(
            stage.at[way, dest],
            land.at[way, dest],
            send.at[way, dest],
            recv.at[way, dest],
            "seq",
            lax.rem(seq + signs[way] + parts, parts),
        )

    def passes(way, dest):
        return seq < dest if way == 0 else seq > dest

    def first(way):
        return seq == 0 if way == 0 else seq == parts - 1

    def forward(way, at):
        dest = parts - 1 - at if way == 0 else at

        @pl.when(passes(way, dest) & first(way))
        def _():
            stage[way, dest] = terms[dest]
            copy(way, dest).start()

        @pl.when(passes(way, dest) & ~first(way))
        def _():
            copy(way, dest).wait_recv()
            stage[way, dest] = (
                terms[dest].astype(F32) + land[way, dest].astype(F32)
            ).astype(stage.dtype)
            copy(way, dest).start()

    def order(lead):
        forward(lead, 0)
        for at in range(parts - 1):
            forward(1 - lead, at)
            if at + 1 < parts - 1:
                forward(lead, at + 1)

    @pl.when(2 * seq < parts)
    def _():
        order(0)

    @pl.when(2 * seq >= parts)
    def _():
        order(1)

    yield
    out[...] = terms[seq].astype(F32)
    for way in range(2):

        @pl.when(~first(way))
        def _():
            copy(way, seq).wait_recv()
            out[...] += land[way, seq].astype(F32)

    for way in range(2):
        for dest in range(parts):

            @pl.when(passes(way, dest))
            def _():
                copy(way, dest).wait_send()


def run(*generators):
    live = list(generators)
    while live:
        live = [item for item in live if next(item, "end") != "end"]


def start_gather(parts, groups, tokens, pieces):
    count = len(pieces)
    half = groups // 2

    def kernel(*refs):
        token_in, piece_in = refs[0], refs[1 : 1 + count]
        token_out, piece_out = refs[1 + count], refs[2 + count : 2 + 2 * count]
        token_send, token_recv, send, recv, pair_send, pair_recv, own = refs[2 + 2 * count :]
        dp = lax.axis_index("dp")
        sibling = dp + 1 - 2 * lax.rem(dp, 2)
        greet((("seq", parts), ("dp", groups)))
        far, near, local = [], [], []
        for k in range(count):
            for step in range(1, half):
                copy = remote(
                    piece_in[k],
                    piece_out[k].at[dp],
                    send.at[k, step],
                    recv.at[k, step],
                    "dp",
                    lax.rem(dp + 2 * step, groups),
                )
                copy.start()
                far.append((k, step, copy))
        line = line_gather(parts, token_in, token_out, token_send, token_recv, own.at[count])
        next(line)
        for k in range(count):
            copy = remote(
                piece_in[k],
                piece_out[k].at[dp],
                pair_send.at[k, 0],
                pair_recv.at[k, 0],
                "dp",
                sibling,
            )
            copy.start()
            near.append(copy)
            copy = pltpu.make_async_copy(piece_in[k], piece_out[k].at[dp], own.at[k])
            copy.start()
            local.append(copy)
        for k, step, copy in far:
            copy.wait_recv()
            origin = lax.rem(dp - 2 * step + groups, groups)
            passed = remote(
                piece_out[k].at[origin],
                piece_out[k].at[origin],
                pair_send.at[k, step],
                pair_recv.at[k, step],
                "dp",
                sibling,
            )
            passed.start()
            near.append(passed)
        for _, _, copy in far:
            copy.wait_send()
        for copy in near + local:
            copy.wait()
        run(line)

    return pl.pallas_call(
        kernel,
        out_shape=[jax.ShapeDtypeStruct((parts,) + tokens.shape, tokens.dtype)]
        + [jax.ShapeDtypeStruct((groups,) + item.shape, item.dtype) for item in pieces],
        in_specs=[ANY] * (1 + count),
        out_specs=[ANY] * (1 + count),
        scratch_shapes=[
            pltpu.SemaphoreType.DMA((2, parts)),
            pltpu.SemaphoreType.DMA((2, parts)),
            pltpu.SemaphoreType.DMA((count, half)),
            pltpu.SemaphoreType.DMA((count, half)),
            pltpu.SemaphoreType.DMA((count, half)),
            pltpu.SemaphoreType.DMA((count, half)),
            pltpu.SemaphoreType.DMA((count + 1,)),
        ],
        compiler_params=params(0),
        name="start_gather",
    )(tokens, *pieces)


def seq_gather(parts, value, collective_id, name):
    def kernel(in_ref, out_ref, send, recv, own):
        greet((("seq", parts),))
        run(line_gather(parts, in_ref, out_ref, send, recv, own))

    return pl.pallas_call(
        kernel,
        out_shape=jax.ShapeDtypeStruct((parts,) + value.shape, value.dtype),
        in_specs=[ANY],
        out_specs=ANY,
        scratch_shapes=[
            pltpu.SemaphoreType.DMA((2, parts)),
            pltpu.SemaphoreType.DMA((2, parts)),
            pltpu.SemaphoreType.DMA,
        ],
        compiler_params=params(collective_id),
        name=name,
    )(value)


def line_scratch(parts, terms):
    return [
        pltpu.VMEM((2,) + terms.shape, terms.dtype),
        pltpu.VMEM((2,) + terms.shape, terms.dtype),
        pltpu.SemaphoreType.DMA((2, parts)),
        pltpu.SemaphoreType.DMA((2, parts)),
    ]


def seq_reduce(parts, terms, collective_id, name):
    def kernel(in_ref, out_ref, stage, land, send, recv):
        greet((("seq", parts),))
        run(line_reduce(parts, in_ref, out_ref, stage, land, send, recv))

    return pl.pallas_call(
        kernel,
        out_shape=jax.ShapeDtypeStruct(terms.shape[1:], F32),
        in_specs=[VMEM],
        out_specs=VMEM,
        scratch_shapes=line_scratch(parts, terms),
        compiler_params=params(collective_id),
        name=name,
    )(terms)


def last_exchange(parts, groups, partial, terms):
    block = terms.shape[1:]

    def kernel(
        partial_in, terms_in, partial_out, sums_out, land, total, send, recv,
        sum_send, sum_recv, own, *line_refs
    ):
        dp = lax.axis_index("dp")
        greet((("seq", parts), ("dp", groups)))
        dp_copies = []
        for step in range(1, groups):
            target = lax.rem(dp + step, groups)
            copy = remote(
                terms_in.at[target], land.at[dp], send.at[step], recv.at[step], "dp", target
            )
            copy.start()
            dp_copies.append(copy)
        line = line_reduce(parts, partial_in, partial_out, *line_refs)
        next(line)
        for copy in dp_copies:
            copy.wait()
        summed = terms_in[dp].astype(F32)
        for step in range(1, groups):
            summed = summed + land[lax.rem(dp + step, groups)].astype(F32)
        total[...] = summed.astype(LOW)
        sums = line_gather(parts, total, sums_out, sum_send, sum_recv, own)
        next(sums)
        run(sums, line)

    dma = pltpu.SemaphoreType.DMA
    return pl.pallas_call(
        kernel,
        out_shape=[
            jax.ShapeDtypeStruct(partial.shape[1:], F32),
            jax.ShapeDtypeStruct((parts,) + block, terms.dtype),
        ],
        in_specs=[VMEM, VMEM],
        out_specs=[VMEM, ANY],
        scratch_shapes=[
            pltpu.VMEM(terms.shape, terms.dtype),
            pltpu.VMEM(block, terms.dtype),
            dma((groups,)),
            dma((groups,)),
            dma((2, parts)),
            dma((2, parts)),
            dma,
        ]
        + line_scratch(parts, partial),
        compiler_params=params(4),
        name="last_exchange",
    )(partial, terms)


def norm_reduce(parts, groups, terms):
    block = terms.shape[1:]

    def kernel(terms_in, out, land, total, seq_land, send, recv, seq_send, seq_recv):
        seq, dp = lax.axis_index("seq"), lax.axis_index("dp")
        greet((("seq", parts), ("dp", groups)))
        copies = []
        for step in range(1, groups):
            target = lax.rem(dp + step, groups)
            copy = remote(
                terms_in.at[target], land.at[dp], send.at[step], recv.at[step], "dp", target
            )
            copy.start()
            copies.append(copy)
        for copy in copies:
            copy.wait()
        summed = terms_in[dp]
        for step in range(1, groups):
            summed = summed + land[lax.rem(dp + step, groups)]
        total[...] = summed
        copies = []
        for step in range(1, parts):
            copy = remote(
                total,
                seq_land.at[seq],
                seq_send.at[step],
                seq_recv.at[step],
                "seq",
                lax.rem(seq + step, parts),
            )
            copy.start()
            copies.append(copy)
        for copy in copies:
            copy.wait()
        for step in range(1, parts):
            summed = summed + seq_land[lax.rem(seq + step, parts)]
        out[...] = summed

    dma = pltpu.SemaphoreType.DMA
    return pl.pallas_call(
        kernel,
        out_shape=jax.ShapeDtypeStruct(block, terms.dtype),
        in_specs=[VMEM],
        out_specs=VMEM,
        scratch_shapes=[
            pltpu.VMEM(terms.shape, terms.dtype),
            pltpu.VMEM(block, terms.dtype),
            pltpu.VMEM((parts,) + block, terms.dtype),
            dma((groups,)),
            dma((groups,)),
            dma((parts,)),
            dma((parts,)),
        ],
        compiler_params=params(5),
        name="norm_reduce",
    )(terms)


def attention_forward(queries, keys, values):
    length, local_width = queries.shape
    heads_here = local_width // HEAD_DIM
    block_rows = min(512, length)
    blocks = length // block_rows
    scale = HEAD_DIM ** (-0.5)
    outs, logs = [], []
    key_index = jnp.arange(length)
    for b in range(blocks):
        seen = (b + 1) * block_rows
        q = queries[b * block_rows : seen].reshape(block_rows, heads_here, HEAD_DIM)
        k = keys[:seen].reshape(seen, heads_here, HEAD_DIM)
        v = values[:seen].reshape(seen, heads_here, HEAD_DIM)
        raw = jnp.einsum("qhd,khd->hqk", q, k, preferred_element_type=F32)
        positions = b * block_rows + jnp.arange(block_rows)
        causal = key_index[None, :seen] <= positions[:, None]
        scores = jnp.where(causal[None], raw * scale, -1e30)
        largest = jnp.max(scores, -1, keepdims=True)
        expo = jnp.exp(scores - largest)
        total = jnp.sum(expo, -1, keepdims=True)
        probs = (expo / total).astype(LOW)
        context = jnp.einsum("hqk,khd->qhd", probs, v, preferred_element_type=F32)
        outs.append(context.astype(LOW).reshape(block_rows, local_width))
        logs.append(largest + jnp.log(total))
    return jnp.concatenate(outs, axis=0), logs


def attention_backward(queries, keys, values, grads, logs):
    length, local_width = queries.shape
    heads_here = local_width // HEAD_DIM
    block_rows = min(512, length)
    blocks = length // block_rows
    scale = HEAD_DIM ** (-0.5)
    key_index = jnp.arange(length)
    query_grads = []
    key_sum = jnp.zeros((length, heads_here, HEAD_DIM), F32)
    value_sum = jnp.zeros((length, heads_here, HEAD_DIM), F32)
    for b in range(blocks):
        seen = (b + 1) * block_rows
        q = queries[b * block_rows : seen].reshape(block_rows, heads_here, HEAD_DIM)
        g = grads[b * block_rows : seen].reshape(block_rows, heads_here, HEAD_DIM)
        k = keys[:seen].reshape(seen, heads_here, HEAD_DIM)
        v = values[:seen].reshape(seen, heads_here, HEAD_DIM)
        raw = jnp.einsum("qhd,khd->hqk", q, k, preferred_element_type=F32)
        positions = b * block_rows + jnp.arange(block_rows)
        causal = key_index[None, :seen] <= positions[:, None]
        scores = jnp.where(causal[None], raw * scale, -1e30)
        probs = jnp.exp(scores - logs[b])
        low_probs = probs.astype(LOW)
        value_term = jnp.einsum("hqk,qhd->khd", low_probs, g, preferred_element_type=F32)
        prob_grad = jnp.einsum("qhd,khd->hqk", g, v, preferred_element_type=F32)
        score_grad = (
            probs * (prob_grad - jnp.sum(probs * prob_grad, -1, keepdims=True))
        ).astype(LOW)
        query_grad = jnp.einsum("hqk,khd->qhd", score_grad, k, preferred_element_type=F32) * scale
        key_term = jnp.einsum("hqk,qhd->khd", score_grad, q, preferred_element_type=F32) * scale
        pad = ((0, length - seen), (0, 0), (0, 0))
        key_sum = key_sum + jnp.pad(key_term, pad)
        value_sum = value_sum + jnp.pad(value_term, pad)
        query_grads.append(query_grad.astype(LOW).reshape(block_rows, local_width))
    return (
        jnp.concatenate(query_grads, axis=0),
        key_sum.astype(LOW).reshape(length, local_width),
        value_sum.astype(LOW).reshape(length, local_width),
    )


def on_device(
    tokens,
    qkv_weight,
    proj_weight,
    hidden_weight,
    output_weight,
    first_gain,
    first_bias,
    second_gain,
    second_bias,
    cotangent,
):
    parts = lax.axis_size("seq")
    groups = lax.axis_size("dp")
    part = lax.axis_index("seq")
    inputs_low = tokens[0]
    rows, width = inputs_low.shape
    model_rows = qkv_weight.shape[0]
    local_width = width // parts
    hidden_rows = output_weight.shape[0] // parts
    hidden_here = hidden_rows * groups

    qkv_here = lax.dynamic_index_in_dim(
        qkv_weight.reshape(model_rows, 3, parts, local_width), part, 2, keepdims=False
    ).reshape(model_rows, 3 * local_width)
    hidden_cols = lax.dynamic_index_in_dim(
        hidden_weight.reshape(model_rows, groups, parts, hidden_rows), part, 2, keepdims=False
    ).reshape(model_rows, hidden_here)
    output_here = lax.dynamic_slice_in_dim(output_weight, part * hidden_rows, hidden_rows, 0)
    direct = model_rows % 16 == 0 and rows % 16 == 0 and groups % 2 == 0
    norms = jnp.stack([first_gain, first_bias, second_gain, second_bias], axis=0)
    if direct:
        pad_lanes = -first_gain.shape[0] % 128
        padded = jnp.pad(norms.astype(F32), ((0, 4), (0, pad_lanes)))
        all_tokens, *pieces = start_gather(
            parts,
            groups,
            inputs_low,
            (qkv_here, padded, proj_weight, hidden_cols, output_here),
        )
        wide_qkv, wide_proj, wide_hidden, wide_output = [
            pieces[at].reshape(groups * pieces[at].shape[1], pieces[at].shape[2])
            for at in (0, 2, 3, 4)
        ]
        norms = pieces[1][:, :4, : first_gain.shape[0]].transpose(1, 0, 2).reshape(4, width)
        all_tokens = all_tokens.reshape(parts * rows, width)
        own_grads, all_tokens = lax.optimization_barrier((cotangent[0], all_tokens))
        all_grads = gather_seq(own_grads)
    else:
        norms = lax.all_gather(norms, "dp", axis=1, tiled=True).astype(F32)
        all_tokens = gather_seq(inputs_low)
        wide_qkv = lax.all_gather(qkv_here, "dp", axis=0, tiled=True)
        wide_proj = lax.all_gather(proj_weight, "dp", axis=0, tiled=True)
        wide_hidden = lax.all_gather(hidden_cols, "dp", axis=0, tiled=True)
        wide_output = lax.all_gather(output_here, "dp", axis=0, tiled=True)
        all_grads = gather_seq(cotangent[0])
    gain_one, bias_one, gain_two, bias_two = norms[0], norms[1], norms[2], norms[3]

    inputs = all_tokens.astype(F32)
    lowered_one = layer_norm(inputs, gain_one, bias_one).astype(LOW)
    projected = matmul(lowered_one, wide_qkv).astype(LOW)
    queries = projected[:, :local_width]
    keys = projected[:, local_width : 2 * local_width]
    values = projected[:, 2 * local_width :]
    context_here, logs = attention_forward(queries, keys, values)
    if direct:
        half = context_here.shape[0] // 2
        folded = jnp.concatenate([context_here[:half], context_here[half:]], axis=1)
        context = seq_gather(parts, folded, 1, "context_gather")
        context = context.reshape(parts, half, 2, local_width).transpose(2, 1, 0, 3)
        context = context.reshape(parts * rows, width)
    else:
        context = lax.all_gather(context_here, "seq", axis=1, tiled=True)
    middle = inputs + matmul(context, wide_proj)
    lowered_two = layer_norm(middle, gain_two, bias_two).astype(LOW)
    hidden_pre = matmul(lowered_two, wide_hidden)
    activated_float, gelu_pull = jax.vjp(gelu_tanh, hidden_pre)
    activated = activated_float.astype(LOW)

    act_grad = matmul_right_t(all_grads, wide_output)
    pre_grad = gelu_pull(act_grad)[0].astype(LOW)
    normed_two_grad = matmul_right_t(pre_grad, wide_hidden)
    if direct:
        normed_two_grad = seq_reduce(
            parts,
            normed_two_grad.astype(LOW).reshape(parts, rows, width),
            2,
            "hidden_reduce",
        )
    else:
        normed_two_grad = scatter_seq(normed_two_grad)
    middle_own = lax.dynamic_slice_in_dim(middle, part * rows, rows, 0)
    _, norm_pull_two = jax.vjp(layer_norm, middle_own, gain_two, bias_two)
    middle_part, gain_two_term, bias_two_term = norm_pull_two(normed_two_grad)
    middle_grad = cotangent[0].astype(F32) + middle_part
    if direct:
        attn_grad = seq_gather(parts, middle_grad.astype(LOW), 3, "attn_gather")
        attn_grad = attn_grad.reshape(parts * rows, width)
    else:
        attn_grad = gather_seq(middle_grad.astype(LOW))

    ffn_terms = matmul(activated, wide_output).astype(LOW)
    ffn_terms, attn_grad = lax.optimization_barrier((ffn_terms, attn_grad))
    block_out = middle_own + scatter_seq(ffn_terms)
    proj_here = lax.dynamic_slice_in_dim(wide_proj, part * local_width, local_width, 0)
    context_grad = matmul_right_t(attn_grad, proj_here).astype(LOW)
    query_grads, key_grads, value_grads = attention_backward(
        queries, keys, values, context_grad, logs
    )
    qkv_grad = jnp.concatenate([query_grads, key_grads, value_grads], axis=1)
    attn_cols = lax.dynamic_slice_in_dim(attn_grad, part * local_width, local_width, 1)
    proj_term = matmul_left_t(context, attn_cols).astype(LOW)
    qkv_term = matmul_left_t(lowered_one, qkv_grad).astype(LOW)
    second_terms = jnp.concatenate([proj_term, qkv_term], axis=1)
    normed_one_grad = matmul_right_t(qkv_grad, wide_qkv)
    if direct:
        normed_one_grad, second_all = last_exchange(
            parts,
            groups,
            normed_one_grad.astype(LOW).reshape(parts, rows, width),
            second_terms.reshape(groups, model_rows, second_terms.shape[1]),
        )
    else:
        normed_one_grad = scatter_seq(normed_one_grad)
        second_sum = lax.psum_scatter(second_terms, "dp", scatter_dimension=0, tiled=True)
        second_all = lax.all_gather(second_sum, "seq", axis=0)
    _, norm_pull_one = jax.vjp(layer_norm, inputs_low.astype(F32), gain_one, bias_one)
    input_part, gain_one_term, bias_one_term = norm_pull_one(normed_one_grad)
    tokens_gradient = (middle_grad + input_part).astype(LOW)

    output_term = matmul_left_t(activated, all_grads).astype(LOW)
    hidden_term = matmul_left_t(lowered_two, pre_grad).astype(LOW)
    first_terms = jnp.concatenate([output_term, hidden_term], axis=1)
    first_sum = lax.psum_scatter(first_terms, "dp", scatter_dimension=0, tiled=True)
    first_all = lax.all_gather(first_sum, "seq", axis=0)
    output_gradient = first_all[:, :, :width].reshape(parts * hidden_rows, width).astype(F32)
    hidden_gradient = (
        first_all[:, :, width:]
        .reshape(parts, model_rows, groups, hidden_rows)
        .transpose(1, 2, 0, 3)
        .reshape(model_rows, parts * hidden_here)
        .astype(F32)
    )
    proj_gradient = (
        second_all[:, :, :local_width].transpose(1, 0, 2).reshape(model_rows, width).astype(F32)
    )
    qkv_gradient = (
        second_all[:, :, local_width:]
        .reshape(parts, model_rows, 3, local_width)
        .transpose(1, 2, 0, 3)
        .reshape(model_rows, 3 * width)
        .astype(F32)
    )
    norm_terms = jnp.stack([gain_one_term, bias_one_term, gain_two_term, bias_two_term], axis=0)
    if direct:
        norm_blocks = norm_terms.reshape(4, groups, model_rows).transpose(1, 0, 2)
        norm_blocks = jnp.pad(norm_blocks, ((0, 0), (0, 4), (0, -model_rows % 128)))
        norm_own = norm_reduce(parts, groups, norm_blocks)[:4, :model_rows]
    else:
        norm_sum = lax.psum(norm_terms, ("seq", "dp"))
        norm_own = lax.dynamic_slice_in_dim(
            norm_sum, lax.axis_index("dp") * model_rows, model_rows, 1
        )
    return (
        block_out.astype(LOW)[None],
        tokens_gradient[None],
        qkv_gradient,
        proj_gradient,
        hidden_gradient,
        output_gradient,
        norm_own[0],
        norm_own[1],
        norm_own[2],
        norm_own[3],
    )


def solution(mesh):
    placed = (
        P("dp", "seq", None),
        P("dp", None),
        P("dp", None),
        P("dp", None),
        P("dp", None),
        P("dp"),
        P("dp"),
        P("dp"),
        P("dp"),
        P("dp", "seq", None),
    )
    return jax.shard_map(
        on_device,
        mesh=mesh,
        in_specs=placed,
        out_specs=(
            P("dp", "seq", None),
            P("dp", "seq", None),
            P("dp", None),
            P("dp", None),
            P("dp", None),
            P("dp", None),
            P("dp"),
            P("dp"),
            P("dp"),
            P("dp"),
        ),
        check_vma=False,
    )
```

```python
import jax
import jax.numpy as jnp
from jax import lax
from jax.experimental import pallas as pl
from jax.experimental.pallas import tpu as pltpu
from jax.sharding import PartitionSpec as P

HEAD_DIM = 64
LOW = jnp.bfloat16
F32 = jnp.float32


def layer_norm(values, gain, bias):
    average = jnp.mean(values, -1, keepdims=True)
    centred = values - average
    variance = jnp.mean(centred * centred, -1, keepdims=True)
    return centred * lax.rsqrt(variance + 1e-05) * gain + bias


def gelu_tanh(values):
    return jax.nn.gelu(values, approximate=True)


def matmul(left, right):
    return jnp.dot(left, right, preferred_element_type=F32)


def matmul_left_t(left, right):
    return lax.dot_general(left, right, (((0,), (0,)), ((), ())), preferred_element_type=F32)


def matmul_right_t(left, right):
    return lax.dot_general(left, right, (((1,), (1,)), ((), ())), preferred_element_type=F32)


def gather_seq(value):
    return lax.all_gather(value, "seq", axis=0, tiled=True)


def scatter_seq(value):
    return lax.psum_scatter(value.astype(LOW), "seq", scatter_dimension=0, tiled=True).astype(F32)


def remote(src, dst, send, recv, axis, target):
    return pltpu.make_async_remote_copy(
        src_ref=src,
        dst_ref=dst,
        send_sem=send,
        recv_sem=recv,
        device_id={axis: target},
        device_id_type=pl.DeviceIdType.MESH,
    )


def greet(axes):
    barrier = pltpu.get_barrier_semaphore()
    count = 0
    for axis, size in axes:
        me = lax.axis_index(axis)
        for step in range(1, size):
            pl.semaphore_signal(
                barrier,
                inc=1,
                device_id={axis: lax.rem(me + step, size)},
                device_id_type=pl.DeviceIdType.MESH,
            )
            count += 1
    pl.semaphore_wait(barrier, count)


ANY = pl.BlockSpec(memory_space=pl.ANY)
VMEM = pl.BlockSpec(memory_space=pltpu.VMEM)


def params(collective_id):
    return pltpu.CompilerParams(
        collective_id=collective_id, has_side_effects=True, vmem_limit_bytes=32 * 1024 * 1024
    )


def line_gather(parts, source, out, send, recv, own):
    seq = lax.axis_index("seq")
    local = pltpu.make_async_copy(source, out.at[seq], own)
    local.start()

    def hop(way, sign, step):
        origin = lax.rem(seq - sign * step + parts, parts)
        return remote(
            source if step == 0 else out.at[origin],
            out.at[origin],
            send.at[way, step],
            recv.at[way, step],
            "seq",
            lax.rem(seq + sign + parts, parts),
        )

    def sends(sign, step):
        origin = seq - sign * step
        return (seq + sign >= 0) & (seq + sign < parts) & (origin >= 0) & (origin < parts)

    def arrives(sign, step):
        origin = seq - sign * step
        return (origin >= 0) & (origin < parts)

    ways = ((0, 1), (1, -1))
    for way, sign in ways:

        @pl.when(sends(sign, 0))
        def _():
            hop(way, sign, 0).start()

    yield
    for step in range(1, parts):
        for way, sign in ways:

            @pl.when(arrives(sign, step))
            def _():
                origin = lax.rem(seq - sign * step + parts, parts)
                remote(
                    source,
                    out.at[origin],
                    send.at[way, step - 1],
                    recv.at[way, step - 1],
                    "seq",
                    lax.rem(seq + sign + parts, parts),
                ).wait_recv()

            if step < parts - 1:

                @pl.when(sends(sign, step))
                def _():
                    hop(way, sign, step).start()

    yield
    for step in range(parts - 1):
        for way, sign in ways:

            @pl.when(sends(sign, step))
            def _():
                hop(way, sign, step).wait_send()

    local.wait()


def line_reduce(parts, terms, out, stage, land, send, recv):
    seq = lax.axis_index("seq")
    signs = (1, -1)

    def copy(way, dest):
        return remote(
            stage.at[way, dest],
            land.at[way, dest],
            send.at[way, dest],
            recv.at[way, dest],
            "seq",
            lax.rem(seq + signs[way] + parts, parts),
        )

    def passes(way, dest):
        return seq < dest if way == 0 else seq > dest

    def first(way):
        return seq == 0 if way == 0 else seq == parts - 1

    def forward(way, at):
        dest = parts - 1 - at if way == 0 else at

        @pl.when(passes(way, dest) & first(way))
        def _():
            stage[way, dest] = terms[dest]
            copy(way, dest).start()

        @pl.when(passes(way, dest) & ~first(way))
        def _():
            copy(way, dest).wait_recv()
            stage[way, dest] = (
                terms[dest].astype(F32) + land[way, dest].astype(F32)
            ).astype(stage.dtype)
            copy(way, dest).start()

    def order(lead):
        forward(lead, 0)
        for at in range(parts - 1):
            forward(1 - lead, at)
            if at + 1 < parts - 1:
                forward(lead, at + 1)

    @pl.when(2 * seq < parts)
    def _():
        order(0)

    @pl.when(2 * seq >= parts)
    def _():
        order(1)

    yield
    out[...] = terms[seq].astype(F32)
    for way in range(2):

        @pl.when(~first(way))
        def _():
            copy(way, seq).wait_recv()
            out[...] += land[way, seq].astype(F32)

    for way in range(2):
        for dest in range(parts):

            @pl.when(passes(way, dest))
            def _():
                copy(way, dest).wait_send()


def run(*generators):
    live = list(generators)
    while live:
        live = [item for item in live if next(item, "end") != "end"]


def start_gather(parts, groups, tokens, pieces):
    count = len(pieces)
    half = groups // 2

    def kernel(*refs):
        token_in, piece_in = refs[0], refs[1 : 1 + count]
        token_out, piece_out = refs[1 + count], refs[2 + count : 2 + 2 * count]
        token_send, token_recv, send, recv, pair_send, pair_recv, own = refs[2 + 2 * count :]
        dp = lax.axis_index("dp")
        sibling = dp + 1 - 2 * lax.rem(dp, 2)
        greet((("seq", parts), ("dp", groups)))
        far, near, local = [], [], []
        for k in range(count):
            for step in range(1, half):
                copy = remote(
                    piece_in[k],
                    piece_out[k].at[dp],
                    send.at[k, step],
                    recv.at[k, step],
                    "dp",
                    lax.rem(dp + 2 * step, groups),
                )
                copy.start()
                far.append((k, step, copy))
        line = line_gather(parts, token_in, token_out, token_send, token_recv, own.at[count])
        next(line)
        for k in range(count):
            copy = remote(
                piece_in[k],
                piece_out[k].at[dp],
                pair_send.at[k, 0],
                pair_recv.at[k, 0],
                "dp",
                sibling,
            )
            copy.start()
            near.append(copy)
            copy = pltpu.make_async_copy(piece_in[k], piece_out[k].at[dp], own.at[k])
            copy.start()
            local.append(copy)
        next(line)
        for k, step, copy in far:
            copy.wait_recv()
            origin = lax.rem(dp - 2 * step + groups, groups)
            passed = remote(
                piece_out[k].at[origin],
                piece_out[k].at[origin],
                pair_send.at[k, step],
                pair_recv.at[k, step],
                "dp",
                sibling,
            )
            passed.start()
            near.append(passed)
        for _, _, copy in far:
            copy.wait_send()
        for copy in near + local:
            copy.wait()
        run(line)

    return pl.pallas_call(
        kernel,
        out_shape=[jax.ShapeDtypeStruct((parts,) + tokens.shape, tokens.dtype)]
        + [jax.ShapeDtypeStruct((groups,) + item.shape, item.dtype) for item in pieces],
        in_specs=[ANY] * (1 + count),
        out_specs=[ANY] * (1 + count),
        scratch_shapes=[
            pltpu.SemaphoreType.DMA((2, parts)),
            pltpu.SemaphoreType.DMA((2, parts)),
            pltpu.SemaphoreType.DMA((count, half)),
            pltpu.SemaphoreType.DMA((count, half)),
            pltpu.SemaphoreType.DMA((count, half)),
            pltpu.SemaphoreType.DMA((count, half)),
            pltpu.SemaphoreType.DMA((count + 1,)),
        ],
        compiler_params=params(0),
        name="start_gather",
    )(tokens, *pieces)


def seq_gather(parts, value, collective_id, name):
    def kernel(in_ref, out_ref, send, recv, own):
        greet((("seq", parts),))
        run(line_gather(parts, in_ref, out_ref, send, recv, own))

    return pl.pallas_call(
        kernel,
        out_shape=jax.ShapeDtypeStruct((parts,) + value.shape, value.dtype),
        in_specs=[ANY],
        out_specs=ANY,
        scratch_shapes=[
            pltpu.SemaphoreType.DMA((2, parts)),
            pltpu.SemaphoreType.DMA((2, parts)),
            pltpu.SemaphoreType.DMA,
        ],
        compiler_params=params(collective_id),
        name=name,
    )(value)


def line_scratch(parts, terms):
    return [
        pltpu.VMEM((2,) + terms.shape, terms.dtype),
        pltpu.VMEM((2,) + terms.shape, terms.dtype),
        pltpu.SemaphoreType.DMA((2, parts)),
        pltpu.SemaphoreType.DMA((2, parts)),
    ]


def seq_reduce(parts, terms, collective_id, name):
    def kernel(in_ref, out_ref, stage, land, send, recv):
        greet((("seq", parts),))
        run(line_reduce(parts, in_ref, out_ref, stage, land, send, recv))

    return pl.pallas_call(
        kernel,
        out_shape=jax.ShapeDtypeStruct(terms.shape[1:], F32),
        in_specs=[VMEM],
        out_specs=VMEM,
        scratch_shapes=line_scratch(parts, terms),
        compiler_params=params(collective_id),
        name=name,
    )(terms)


def last_exchange(parts, groups, partial, terms):
    block = terms.shape[1:]

    def kernel(
        partial_in, terms_in, partial_out, sums_out, land, total, send, recv,
        sum_send, sum_recv, own, *line_refs
    ):
        dp = lax.axis_index("dp")
        greet((("seq", parts), ("dp", groups)))
        dp_copies = []
        for step in range(1, groups):
            target = lax.rem(dp + step, groups)
            copy = remote(
                terms_in.at[target], land.at[dp], send.at[step], recv.at[step], "dp", target
            )
            copy.start()
            dp_copies.append(copy)
        line = line_reduce(parts, partial_in, partial_out, *line_refs)
        next(line)
        for copy in dp_copies:
            copy.wait()
        summed = terms_in[dp].astype(F32)
        for step in range(1, groups):
            summed = summed + land[lax.rem(dp + step, groups)].astype(F32)
        total[...] = summed.astype(LOW)
        sums = line_gather(parts, total, sums_out, sum_send, sum_recv, own)
        next(sums)
        run(sums, line)

    dma = pltpu.SemaphoreType.DMA
    return pl.pallas_call(
        kernel,
        out_shape=[
            jax.ShapeDtypeStruct(partial.shape[1:], F32),
            jax.ShapeDtypeStruct((parts,) + block, terms.dtype),
        ],
        in_specs=[VMEM, VMEM],
        out_specs=[VMEM, ANY],
        scratch_shapes=[
            pltpu.VMEM(terms.shape, terms.dtype),
            pltpu.VMEM(block, terms.dtype),
            dma((groups,)),
            dma((groups,)),
            dma((2, parts)),
            dma((2, parts)),
            dma,
        ]
        + line_scratch(parts, partial),
        compiler_params=params(4),
        name="last_exchange",
    )(partial, terms)


def norm_reduce(parts, groups, terms):
    block = terms.shape[1:]

    def kernel(terms_in, out, land, total, seq_land, send, recv, seq_send, seq_recv):
        seq, dp = lax.axis_index("seq"), lax.axis_index("dp")
        greet((("seq", parts), ("dp", groups)))
        copies = []
        for step in range(1, groups):
            target = lax.rem(dp + step, groups)
            copy = remote(
                terms_in.at[target], land.at[dp], send.at[step], recv.at[step], "dp", target
            )
            copy.start()
            copies.append(copy)
        for copy in copies:
            copy.wait()
        summed = terms_in[dp]
        for step in range(1, groups):
            summed = summed + land[lax.rem(dp + step, groups)]
        total[...] = summed
        copies = []
        for step in range(1, parts):
            copy = remote(
                total,
                seq_land.at[seq],
                seq_send.at[step],
                seq_recv.at[step],
                "seq",
                lax.rem(seq + step, parts),
            )
            copy.start()
            copies.append(copy)
        for copy in copies:
            copy.wait()
        for step in range(1, parts):
            summed = summed + seq_land[lax.rem(seq + step, parts)]
        out[...] = summed

    dma = pltpu.SemaphoreType.DMA
    return pl.pallas_call(
        kernel,
        out_shape=jax.ShapeDtypeStruct(block, terms.dtype),
        in_specs=[VMEM],
        out_specs=VMEM,
        scratch_shapes=[
            pltpu.VMEM(terms.shape, terms.dtype),
            pltpu.VMEM(block, terms.dtype),
            pltpu.VMEM((parts,) + block, terms.dtype),
            dma((groups,)),
            dma((groups,)),
            dma((parts,)),
            dma((parts,)),
        ],
        compiler_params=params(5),
        name="norm_reduce",
    )(terms)


def attention_forward(queries, keys, values):
    length, local_width = queries.shape
    heads_here = local_width // HEAD_DIM
    block_rows = min(512, length)
    blocks = length // block_rows
    scale = HEAD_DIM ** (-0.5)
    outs, logs = [], []
    key_index = jnp.arange(length)
    for b in range(blocks):
        seen = (b + 1) * block_rows
        q = queries[b * block_rows : seen].reshape(block_rows, heads_here, HEAD_DIM)
        k = keys[:seen].reshape(seen, heads_here, HEAD_DIM)
        v = values[:seen].reshape(seen, heads_here, HEAD_DIM)
        raw = jnp.einsum("qhd,khd->hqk", q, k, preferred_element_type=F32)
        positions = b * block_rows + jnp.arange(block_rows)
        causal = key_index[None, :seen] <= positions[:, None]
        scores = jnp.where(causal[None], raw * scale, -1e30)
        largest = jnp.max(scores, -1, keepdims=True)
        expo = jnp.exp(scores - largest)
        total = jnp.sum(expo, -1, keepdims=True)
        probs = (expo / total).astype(LOW)
        context = jnp.einsum("hqk,khd->qhd", probs, v, preferred_element_type=F32)
        outs.append(context.astype(LOW).reshape(block_rows, local_width))
        logs.append(largest + jnp.log(total))
    return jnp.concatenate(outs, axis=0), logs


def attention_backward(queries, keys, values, grads, logs):
    length, local_width = queries.shape
    heads_here = local_width // HEAD_DIM
    block_rows = min(512, length)
    blocks = length // block_rows
    scale = HEAD_DIM ** (-0.5)
    key_index = jnp.arange(length)
    query_grads = []
    key_sum = jnp.zeros((length, heads_here, HEAD_DIM), F32)
    value_sum = jnp.zeros((length, heads_here, HEAD_DIM), F32)
    for b in range(blocks):
        seen = (b + 1) * block_rows
        q = queries[b * block_rows : seen].reshape(block_rows, heads_here, HEAD_DIM)
        g = grads[b * block_rows : seen].reshape(block_rows, heads_here, HEAD_DIM)
        k = keys[:seen].reshape(seen, heads_here, HEAD_DIM)
        v = values[:seen].reshape(seen, heads_here, HEAD_DIM)
        raw = jnp.einsum("qhd,khd->hqk", q, k, preferred_element_type=F32)
        positions = b * block_rows + jnp.arange(block_rows)
        causal = key_index[None, :seen] <= positions[:, None]
        scores = jnp.where(causal[None], raw * scale, -1e30)
        probs = jnp.exp(scores - logs[b])
        low_probs = probs.astype(LOW)
        value_term = jnp.einsum("hqk,qhd->khd", low_probs, g, preferred_element_type=F32)
        prob_grad = jnp.einsum("qhd,khd->hqk", g, v, preferred_element_type=F32)
        score_grad = (
            probs * (prob_grad - jnp.sum(probs * prob_grad, -1, keepdims=True))
        ).astype(LOW)
        query_grad = jnp.einsum("hqk,khd->qhd", score_grad, k, preferred_element_type=F32) * scale
        key_term = jnp.einsum("hqk,qhd->khd", score_grad, q, preferred_element_type=F32) * scale
        pad = ((0, length - seen), (0, 0), (0, 0))
        key_sum = key_sum + jnp.pad(key_term, pad)
        value_sum = value_sum + jnp.pad(value_term, pad)
        query_grads.append(query_grad.astype(LOW).reshape(block_rows, local_width))
    return (
        jnp.concatenate(query_grads, axis=0),
        key_sum.astype(LOW).reshape(length, local_width),
        value_sum.astype(LOW).reshape(length, local_width),
    )


def on_device(
    tokens,
    qkv_weight,
    proj_weight,
    hidden_weight,
    output_weight,
    first_gain,
    first_bias,
    second_gain,
    second_bias,
    cotangent,
):
    parts = lax.axis_size("seq")
    groups = lax.axis_size("dp")
    part = lax.axis_index("seq")
    inputs_low = tokens[0]
    rows, width = inputs_low.shape
    model_rows = qkv_weight.shape[0]
    local_width = width // parts
    hidden_rows = output_weight.shape[0] // parts
    hidden_here = hidden_rows * groups

    qkv_here = lax.dynamic_index_in_dim(
        qkv_weight.reshape(model_rows, 3, parts, local_width), part, 2, keepdims=False
    ).reshape(model_rows, 3 * local_width)
    hidden_cols = lax.dynamic_index_in_dim(
        hidden_weight.reshape(model_rows, groups, parts, hidden_rows), part, 2, keepdims=False
    ).reshape(model_rows, hidden_here)
    output_here = lax.dynamic_slice_in_dim(output_weight, part * hidden_rows, hidden_rows, 0)
    direct = model_rows % 16 == 0 and rows % 16 == 0 and groups % 2 == 0
    norms = jnp.stack([first_gain, first_bias, second_gain, second_bias], axis=0)
    if direct:
        pad_lanes = -first_gain.shape[0] % 128
        padded = jnp.pad(norms.astype(F32), ((0, 4), (0, pad_lanes)))
        all_tokens, *pieces = start_gather(
            parts,
            groups,
            inputs_low,
            (qkv_here, padded, proj_weight, hidden_cols, output_here),
        )
        wide_qkv, wide_proj, wide_hidden, wide_output = [
            pieces[at].reshape(groups * pieces[at].shape[1], pieces[at].shape[2])
            for at in (0, 2, 3, 4)
        ]
        norms = pieces[1][:, :4, : first_gain.shape[0]].transpose(1, 0, 2).reshape(4, width)
        all_tokens = all_tokens.reshape(parts * rows, width)
        own_grads, all_tokens = lax.optimization_barrier((cotangent[0], all_tokens))
        all_grads = gather_seq(own_grads)
    else:
        norms = lax.all_gather(norms, "dp", axis=1, tiled=True).astype(F32)
        all_tokens = gather_seq(inputs_low)
        wide_qkv = lax.all_gather(qkv_here, "dp", axis=0, tiled=True)
        wide_proj = lax.all_gather(proj_weight, "dp", axis=0, tiled=True)
        wide_hidden = lax.all_gather(hidden_cols, "dp", axis=0, tiled=True)
        wide_output = lax.all_gather(output_here, "dp", axis=0, tiled=True)
        all_grads = gather_seq(cotangent[0])
    gain_one, bias_one, gain_two, bias_two = norms[0], norms[1], norms[2], norms[3]

    inputs = all_tokens.astype(F32)
    lowered_one = layer_norm(inputs, gain_one, bias_one).astype(LOW)
    projected = matmul(lowered_one, wide_qkv).astype(LOW)
    queries = projected[:, :local_width]
    keys = projected[:, local_width : 2 * local_width]
    values = projected[:, 2 * local_width :]
    context_here, logs = attention_forward(queries, keys, values)
    if direct:
        half = context_here.shape[0] // 2
        folded = jnp.concatenate([context_here[:half], context_here[half:]], axis=1)
        context = seq_gather(parts, folded, 1, "context_gather")
        context = context.reshape(parts, half, 2, local_width).transpose(2, 1, 0, 3)
        context = context.reshape(parts * rows, width)
    else:
        context = lax.all_gather(context_here, "seq", axis=1, tiled=True)
    middle = inputs + matmul(context, wide_proj)
    lowered_two = layer_norm(middle, gain_two, bias_two).astype(LOW)
    hidden_pre = matmul(lowered_two, wide_hidden)
    activated_float, gelu_pull = jax.vjp(gelu_tanh, hidden_pre)
    activated = activated_float.astype(LOW)

    act_grad = matmul_right_t(all_grads, wide_output)
    pre_grad = gelu_pull(act_grad)[0].astype(LOW)
    normed_two_grad = matmul_right_t(pre_grad, wide_hidden)
    if direct:
        normed_two_grad = seq_reduce(
            parts,
            normed_two_grad.astype(LOW).reshape(parts, rows, width),
            2,
            "hidden_reduce",
        )
    else:
        normed_two_grad = scatter_seq(normed_two_grad)
    middle_own = lax.dynamic_slice_in_dim(middle, part * rows, rows, 0)
    _, norm_pull_two = jax.vjp(layer_norm, middle_own, gain_two, bias_two)
    middle_part, gain_two_term, bias_two_term = norm_pull_two(normed_two_grad)
    middle_grad = cotangent[0].astype(F32) + middle_part
    if direct:
        attn_grad = seq_gather(parts, middle_grad.astype(LOW), 3, "attn_gather")
        attn_grad = attn_grad.reshape(parts * rows, width)
    else:
        attn_grad = gather_seq(middle_grad.astype(LOW))

    ffn_terms = matmul(activated, wide_output).astype(LOW)
    ffn_terms, attn_grad = lax.optimization_barrier((ffn_terms, attn_grad))
    block_out = middle_own + scatter_seq(ffn_terms)
    proj_here = lax.dynamic_slice_in_dim(wide_proj, part * local_width, local_width, 0)
    context_grad = matmul_right_t(attn_grad, proj_here).astype(LOW)
    query_grads, key_grads, value_grads = attention_backward(
        queries, keys, values, context_grad, logs
    )
    qkv_grad = jnp.concatenate([query_grads, key_grads, value_grads], axis=1)
    attn_cols = lax.dynamic_slice_in_dim(attn_grad, part * local_width, local_width, 1)
    proj_term = matmul_left_t(context, attn_cols).astype(LOW)
    qkv_term = matmul_left_t(lowered_one, qkv_grad).astype(LOW)
    second_terms = jnp.concatenate([proj_term, qkv_term], axis=1)
    normed_one_grad = matmul_right_t(qkv_grad, wide_qkv)
    if direct:
        normed_one_grad, second_all = last_exchange(
            parts,
            groups,
            normed_one_grad.astype(LOW).reshape(parts, rows, width),
            second_terms.reshape(groups, model_rows, second_terms.shape[1]),
        )
    else:
        normed_one_grad = scatter_seq(normed_one_grad)
        second_sum = lax.psum_scatter(second_terms, "dp", scatter_dimension=0, tiled=True)
        second_all = lax.all_gather(second_sum, "seq", axis=0)
    _, norm_pull_one = jax.vjp(layer_norm, inputs_low.astype(F32), gain_one, bias_one)
    input_part, gain_one_term, bias_one_term = norm_pull_one(normed_one_grad)
    tokens_gradient = (middle_grad + input_part).astype(LOW)

    output_term = matmul_left_t(activated, all_grads).astype(LOW)
    hidden_term = matmul_left_t(lowered_two, pre_grad).astype(LOW)
    first_terms = jnp.concatenate([output_term, hidden_term], axis=1)
    first_sum = lax.psum_scatter(first_terms, "dp", scatter_dimension=0, tiled=True)
    first_all = lax.all_gather(first_sum, "seq", axis=0)
    output_gradient = first_all[:, :, :width].reshape(parts * hidden_rows, width).astype(F32)
    hidden_gradient = (
        first_all[:, :, width:]
        .reshape(parts, model_rows, groups, hidden_rows)
        .transpose(1, 2, 0, 3)
        .reshape(model_rows, parts * hidden_here)
        .astype(F32)
    )
    proj_gradient = (
        second_all[:, :, :local_width].transpose(1, 0, 2).reshape(model_rows, width).astype(F32)
    )
    qkv_gradient = (
        second_all[:, :, local_width:]
        .reshape(parts, model_rows, 3, local_width)
        .transpose(1, 2, 0, 3)
        .reshape(model_rows, 3 * width)
        .astype(F32)
    )
    norm_terms = jnp.stack([gain_one_term, bias_one_term, gain_two_term, bias_two_term], axis=0)
    if direct:
        norm_blocks = norm_terms.reshape(4, groups, model_rows).transpose(1, 0, 2)
        norm_blocks = jnp.pad(norm_blocks, ((0, 0), (0, 4), (0, -model_rows % 128)))
        norm_own = norm_reduce(parts, groups, norm_blocks)[:4, :model_rows]
    else:
        norm_sum = lax.psum(norm_terms, ("seq", "dp"))
        norm_own = lax.dynamic_slice_in_dim(
            norm_sum, lax.axis_index("dp") * model_rows, model_rows, 1
        )
    return (
        block_out.astype(LOW)[None],
        tokens_gradient[None],
        qkv_gradient,
        proj_gradient,
        hidden_gradient,
        output_gradient,
        norm_own[0],
        norm_own[1],
        norm_own[2],
        norm_own[3],
    )


def solution(mesh):
    placed = (
        P("dp", "seq", None),
        P("dp", None),
        P("dp", None),
        P("dp", None),
        P("dp", None),
        P("dp"),
        P("dp"),
        P("dp"),
        P("dp"),
        P("dp", "seq", None),
    )
    return jax.shard_map(
        on_device,
        mesh=mesh,
        in_specs=placed,
        out_specs=(
            P("dp", "seq", None),
            P("dp", "seq", None),
            P("dp", None),
            P("dp", None),
            P("dp", None),
            P("dp", None),
            P("dp"),
            P("dp"),
            P("dp"),
            P("dp"),
        ),
        check_vma=False,
    )
```
